768 devices in a mesh: fsdp: 96 (over z_hi, x, y), tensor: 8 (over z_lo, core).
Axes of the slice: x: 4, y: 8, z: 12 (z_hi: 3, z_lo: 4; z = z_hi * 4 + z_lo), core: 2. Of those that a mesh axis runs over, the one named last changes fastest.
Arguments:
- out_grad: bfloat16 [98304, 2048], P(('fsdp', 'tensor')), may hold values from -6 to 6
- hidden: bfloat16 [98304, 3072], P('fsdp', 'tensor'), may hold values from -6 to 6
- segments: int32 [96, 1024], P('fsdp'), may hold values from 0 to 7, never falling along the last dimension, each value on 1 to 512 neighbouring positions
- master: float32 [3072, 2048], P(('tensor', 'fsdp')), may hold values from -0.078125 to 0.078125
- moment_one: float32 [3072, 2048], P(('tensor', 'fsdp')), may hold values from -0.15625 to 0.15625
- moment_two: float32 [3072, 2048], P(('tensor', 'fsdp')), may hold values from 1e-05 to 0.001
- step_count: int32 [], replicated, may hold values from 1 to 40
- layer_one: bfloat16 [3072, 2048], P(('tensor', 'fsdp')), may hold values from -0.078125 to 0.078125
Outputs:
- hidden_grad: bfloat16 [98304, 3072], P('fsdp', 'tensor')
- new_master: float32 [3072, 2048], P(('tensor', 'fsdp'))
- new_moment_one: float32 [3072, 2048], P(('tensor', 'fsdp'))
- new_moment_two: float32 [3072, 2048], P(('tensor', 'fsdp'))
- update: float32 [3072, 2048], P(('tensor', 'fsdp'))
- layer_one_rows: bfloat16 [3072, 2048], P('tensor')
The draws below stay inside these ranges and needn't reach their ends.
Inputs may be any that keep to these rules, and one draw needn't show every extreme that they name: `segments`: within a row document numbers never fall and every document has at least one token; some document has exactly 512 tokens.
All inputs are finite; a program needn't handle non-finite values.
Results may differ from the reference program's by a relative error of at most 0.0055.
Values may be sent and summed in bfloat16 or wider, within the bound.
No kernel may reach another device: no remote copies, remote signals or barrier semaphores. Data moves between devices by JAX's collectives and lax.ppermute only.
A program may use at most 64 MiB of HBM per device.

```python
import math
import jax
import jax.numpy as jnp
import numpy as np
from jax import lax

D = 2048
FF = 5632
TOK_DEV = 1024
DOCS = 8
FF_WIN = 3072
TOKENS = 98304
GROUPS = 96
N_FSDP = 96


def levels(rng, extent, pieces, least, top_value):
    factor_of, own = 1.0, jax.random.fold_in(rng, 6)
    for axis_at, blocks in pieces:
        heights = jnp.exp(jax.random.uniform(jax.random.fold_in(own, axis_at), (blocks,), jnp.float32, least / len(pieces), top_value / len(pieces)))
        factor_of = factor_of * jnp.repeat(heights, extent[axis_at] // blocks).reshape([-1 if axis == axis_at else 1 for axis in range(len(extent))])
    return factor_of


def profile(count, total, reach, lean):
    weights = [(1 << 20) // math.isqrt(grade ** lean) + 1 for grade in range(2, count + 1)]
    rest, given = total - reach - (count - 1), [1] * (count - 1)
    while rest > 0:
        free = [i for i in range(count - 1) if given[i] < reach]
        whole, left = sum([weights[i] for i in free]), rest
        for i in free:
            extra = min(reach - given[i], max(1, left * weights[i] // whole), rest)
            given[i] = given[i] + extra
            rest = rest - extra
    return np.array([reach] + given)


def ragged_sizes(rng, amount, total, bound, lean):
    if amount == 2:
        one = jax.random.randint(rng, (), max(1, total - bound), min(bound, total - 1) + 1)
        return jnp.stack([one, total - one])
    lengths = jnp.asarray(profile(amount, total, bound, lean), jnp.int32)
    twos = (amount - 1) // 2
    source_of, receiver = lengths[1:1 + 2 * twos:2], lengths[2:2 + 2 * twos:2]
    margin = jnp.minimum(source_of - 1, bound - receiver)
    moved = jax.random.randint(jax.random.fold_in(rng, 1), (twos,), 0, 1 << 20) % (margin + 1)
    lengths = lengths.at[1:1 + 2 * twos:2].set(source_of - moved).at[2:2 + 2 * twos:2].set(receiver + moved)
    return lengths[jax.random.permutation(jax.random.fold_in(rng, 2), amount)]


def gaussian(own_key, dims, width, most, split=(), held_as=jnp.bfloat16):
    entries = width * jax.random.normal(own_key, dims, jnp.float32)
    if split:
        entries = entries * levels(own_key, dims, split, -0.22, 0.18)
    return jnp.clip(entries, -most, most).astype(held_as)


def setup_inputs(seed: int = 0) -> dict:
    key_of = jax.random.split(jax.random.key(seed), 9)
    out_grad = gaussian(key_of[0], (TOKENS, D), 1.0, 6.0, ((0, 768),))
    hidden = gaussian(key_of[1], (TOKENS, FF_WIN), 1.0, 6.0, ((0, 96), (1, 8)))
    segments = jax.vmap(lambda own: jnp.searchsorted(jnp.cumsum(ragged_sizes(own, DOCS, TOK_DEV, TOK_DEV // 2, 2)), jnp.arange(TOK_DEV), side="right"))(jax.random.split(key_of[2], GROUPS)).reshape((GROUPS, TOK_DEV)).astype(jnp.int32)
    master = gaussian(key_of[3], (FF_WIN, D), FF ** -0.5, 0.078125, ((0, 768),), jnp.float32)
    moment_one = gaussian(key_of[4], (FF_WIN, D), 0.01, 0.15625, ((0, 768),), jnp.float32)
    moment_two = jnp.clip(jnp.exp(math.log(0.001) - 4.6051703 * jax.random.uniform(key_of[5], (FF_WIN, D), jnp.float32) ** levels(key_of[5], (FF_WIN, D), ((0, 768),), -0.2, 0.2)), 9.999999747378752e-06, 0.001)
    step_count = jax.random.randint(key_of[6], (), 1, 41).astype(jnp.int32)
    layer_one = gaussian(key_of[7], (FF_WIN, D), FF ** -0.5, 0.078125, ((0, 768),))
    return {"out_grad": out_grad, "hidden": hidden, "segments": segments, "master": master, "moment_one": moment_one, "moment_two": moment_two, "step_count": step_count, "layer_one": layer_one}


def reference(out_grad, hidden, segments, master, moment_one, moment_two, step_count, layer_one):
    all_tokens = TOK_DEV * N_FSDP
    same_doc = (segments[:, :, None] == segments[:, None, :]).astype(jnp.float32)
    doc_len = lax.optimization_barrier(jnp.sum(same_doc, axis=2)).reshape(all_tokens)
    weight = TOK_DEV / DOCS / doc_len
    scaled = (out_grad.astype(jnp.float32) * weight[:, None]).astype(jnp.bfloat16)
    last_weights = master.astype(jnp.bfloat16)
    hidden_grad = lax.dot_general(scaled, last_weights, (((1,), (1,)), ((), ())), preferred_element_type=jnp.float32).astype(jnp.bfloat16)
    gradient = lax.dot_general(hidden, scaled, (((0,), (0,)), ((), ())), preferred_element_type=jnp.float32) / all_tokens
    new_moment_one = 0.9 * moment_one + 0.1 * gradient
    new_moment_two = 0.95 * moment_two + 0.05 * gradient * gradient
    step_float = step_count.astype(jnp.float32)
    first_fix = 1.0 - jnp.power(jnp.float32(0.9), step_float)
    second_fix = 1.0 - jnp.power(jnp.float32(0.95), step_float)
    update = new_moment_one / first_fix / (jnp.sqrt(new_moment_two / second_fix) + 1e-08) + 0.1 * master
    new_master = master - 0.00015 * update
    return (hidden_grad, new_master, new_moment_one, new_moment_two, update, layer_one)
```

```python
import jax
import jax.numpy as jnp
from jax import lax
from jax.sharding import Mesh
from jax.sharding import PartitionSpec as P

DOCS = 8
BF = jnp.bfloat16
F32 = jnp.float32


def spread(block, axes, size):
    return lax.all_to_all(jnp.broadcast_to(block[None], (size,) + block.shape), axes, 0, 0)


def per_device(out_grad, hidden, segments, master, moment_one, moment_two, step_count, layer_one):
    n_zh, n_x, n_yh, n_yl = [lax.axis_size(a) for a in ("zh", "x", "yh", "yl")]
    n_y = n_yh * n_yl
    rows, width = master.shape
    tok_dev, units = hidden.shape
    all_tokens = tok_dev * n_zh * n_x * n_y

    with jax.named_scope("gather_grads"):
        full_grads = lax.all_gather(out_grad, ("zl", "c"), axis=0, tiled=True)

    with jax.named_scope("gather_weights"):
        pair = jnp.stack([master.astype(BF), layer_one])
        pair = spread(pair, "zh", n_zh)
        pair = spread(pair, ("yh", "yl"), n_y)
        pair = pair.transpose(2, 1, 0, 3, 4).reshape(2, n_zh * n_y * rows, width)
        last = spread(pair[0], "x", n_x)
        first = lax.all_gather(pair[1], "x", axis=0, tiled=False)

    def in_order(w):
        return w.reshape(n_x, n_zh, n_y * rows, width).transpose(1, 0, 2, 3).reshape(units, width)

    with jax.named_scope("weights_of_tokens"):
        seg_row = segments[0]
        same_doc = (seg_row[:, None] == seg_row[None, :]).astype(F32)
        doc_len = jnp.sum(same_doc, axis=1)
        weight = tok_dev / DOCS / doc_len
        scaled = (full_grads.astype(F32) * weight[:, None]).astype(BF)

    with jax.named_scope("unit_order"):
        place = jnp.arange(units, dtype=jnp.int32).reshape(n_zh, n_x, n_yh, n_yl, rows)
        place = place.transpose(1, 3, 0, 2, 4).reshape(units)
        pick = (jnp.arange(units, dtype=jnp.int32)[:, None] == place[None, :]).astype(BF)
        ordered = lax.dot_general(
            hidden, pick, (((1,), (0,)), ((), ())), preferred_element_type=F32
        ).astype(BF)

    with jax.named_scope("gradient"):
        grad_local = lax.dot_general(
            ordered, scaled, (((0,), (0,)), ((), ())), preferred_element_type=F32
        ).astype(BF)
        parts = lax.all_to_all(
            grad_local.reshape(n_x * n_yl, units // (n_x * n_yl), width), ("x", "yl"), 0, 0
        )
        part = jnp.sum(parts.astype(F32), axis=0).astype(BF)
        parts = lax.all_to_all(part.reshape(n_zh * n_yh, rows, width), ("zh", "yh"), 0, 0)
        gradient = jnp.sum(parts.astype(F32), axis=0)

    with jax.named_scope("hidden_grad"):
        hidden_grad = lax.dot_general(
            scaled, in_order(last), (((1,), (1,)), ((), ())), preferred_element_type=F32
        )

    with jax.named_scope("adamw"):
        gradient = gradient / all_tokens
        new_moment_one = 0.9 * moment_one + 0.1 * gradient
        new_moment_two = 0.95 * moment_two + 0.05 * gradient * gradient
        step_float = step_count.astype(F32)
        first_fix = 1.0 - jnp.power(F32(0.9), step_float)
        second_fix = 1.0 - jnp.power(F32(0.95), step_float)
        update = (
            new_moment_one / first_fix / (jnp.sqrt(new_moment_two / second_fix) + 1e-08)
            + 0.1 * master
        )
        new_master = master - 0.00015 * update
    return (
        hidden_grad.astype(BF),
        new_master,
        new_moment_one,
        new_moment_two,
        update,
        in_order(first),
    )


def solution(mesh):
    fine = Mesh(mesh.devices.reshape(3, 4, 4, 2, 4, 2), ("zh", "x", "yh", "yl", "zl", "c"))
    fsdp = ("zh", "x", "yh", "yl")
    tensor = ("zl", "c")
    in_specs = (
        P(fsdp + tensor, None),
        P(fsdp, tensor),
        P(fsdp, None),
        P(tensor + fsdp, None),
        P(tensor + fsdp, None),
        P(tensor + fsdp, None),
        P(),
        P(tensor + fsdp, None),
    )
    out_specs = (
        P(fsdp, tensor),
        P(tensor + fsdp, None),
        P(tensor + fsdp, None),
        P(tensor + fsdp, None),
        P(tensor + fsdp, None),
        P(tensor, None),
    )
    return jax.shard_map(
        per_device, mesh=fine, in_specs=in_specs, out_specs=out_specs, check_vma=False
    )
```

```python
import jax
import jax.numpy as jnp
from jax import lax
from jax.sharding import Mesh
from jax.sharding import PartitionSpec as P

DOCS = 8
BF = jnp.bfloat16
F32 = jnp.float32


def spread(block, axes, size):
    return lax.all_to_all(jnp.broadcast_to(block[None], (size,) + block.shape), axes, 0, 0)


def per_device(out_grad, hidden, segments, master, moment_one, moment_two, step_count, layer_one):
    n_zh, n_x, n_yh, n_yl = [lax.axis_size(a) for a in ("zh", "x", "yh", "yl")]
    n_y = n_yh * n_yl
    rows, width = master.shape
    tok_dev, units = hidden.shape
    all_tokens = tok_dev * n_zh * n_x * n_y

    with jax.named_scope("gather_grads"):
        full_grads = lax.all_gather(out_grad, ("zl", "c"), axis=0, tiled=True)

    with jax.named_scope("gather_weights"):
        pair = jnp.stack([master.astype(BF), layer_one])
        pair = spread(pair, "zh", n_zh)
        pair = spread(pair, ("yh", "yl"), n_y)
        pair = pair.transpose(2, 1, 0, 3, 4).reshape(2, n_zh * n_y * rows, width)
        last = spread(pair[0], "x", n_x)
        full_grads, last = lax.optimization_barrier((full_grads, last))

    def in_order(w):
        return w.reshape(n_x, n_zh, n_y * rows, width).transpose(1, 0, 2, 3).reshape(units, width)

    with jax.named_scope("weights_of_tokens"):
        seg_row = segments[0]
        same_doc = (seg_row[:, None] == seg_row[None, :]).astype(F32)
        doc_len = jnp.sum(same_doc, axis=1)
        weight = tok_dev / DOCS / doc_len
        scaled = (full_grads.astype(F32) * weight[:, None]).astype(BF)

    with jax.named_scope("unit_order"):
        place = jnp.arange(units, dtype=jnp.int32).reshape(n_zh, n_x, n_yh, n_yl, rows)
        place = place.transpose(1, 3, 0, 2, 4).reshape(units)
        pick = (jnp.arange(units, dtype=jnp.int32)[:, None] == place[None, :]).astype(BF)
        ordered = lax.dot_general(
            hidden, pick, (((1,), (0,)), ((), ())), preferred_element_type=F32
        ).astype(BF)

    with jax.named_scope("gradient"):
        grad_local = lax.dot_general(
            ordered, scaled, (((0,), (0,)), ((), ())), preferred_element_type=F32
        ).astype(BF)
        parts = lax.all_to_all(
            grad_local.reshape(n_x * n_yl, units // (n_x * n_yl), width), ("x", "yl"), 0, 0
        )
        parts, rest = lax.optimization_barrier((parts, pair[1]))
        part = jnp.sum(parts.astype(F32), axis=0).astype(BF)
        first = lax.all_gather(rest, "x", axis=0, tiled=False)
        parts = lax.all_to_all(part.reshape(n_zh * n_yh, rows, width), ("zh", "yh"), 0, 0)
        gradient = jnp.sum(parts.astype(F32), axis=0)

    with jax.named_scope("hidden_grad"):
        hidden_grad = lax.dot_general(
            scaled, in_order(last), (((1,), (1,)), ((), ())), preferred_element_type=F32
        )

    with jax.named_scope("adamw"):
        gradient = gradient / all_tokens
        new_moment_one = 0.9 * moment_one + 0.1 * gradient
        new_moment_two = 0.95 * moment_two + 0.05 * gradient * gradient
        step_float = step_count.astype(F32)
        first_fix = 1.0 - jnp.power(F32(0.9), step_float)
        second_fix = 1.0 - jnp.power(F32(0.95), step_float)
        update = (
            new_moment_one / first_fix / (jnp.sqrt(new_moment_two / second_fix) + 1e-08)
            + 0.1 * master
        )
        new_master = master - 0.00015 * update
    return (
        hidden_grad.astype(BF),
        new_master,
        new_moment_one,
        new_moment_two,
        update,
        in_order(first),
    )


def solution(mesh):
    fine = Mesh(mesh.devices.reshape(3, 4, 4, 2, 4, 2), ("zh", "x", "yh", "yl", "zl", "c"))
    fsdp = ("zh", "x", "yh", "yl")
    tensor = ("zl", "c")
    in_specs = (
        P(fsdp + tensor, None),
        P(fsdp, tensor),
        P(fsdp, None),
        P(tensor + fsdp, None),
        P(tensor + fsdp, None),
        P(tensor + fsdp, None),
        P(),
        P(tensor + fsdp, None),
    )
    out_specs = (
        P(fsdp, tensor),
        P(tensor + fsdp, None),
        P(tensor + fsdp, None),
        P(tensor + fsdp, None),
        P(tensor + fsdp, None),
        P(tensor, None),
    )
    return jax.shard_map(
        per_device, mesh=fine, in_specs=in_specs, out_specs=out_specs, check_vma=False
    )
```

```python
import jax
import jax.numpy as jnp
from jax import lax
from jax.experimental import pallas as pl
from jax.experimental.pallas import tpu as pltpu
from jax.sharding import Mesh
from jax.sharding import PartitionSpec as P

DOCS = 8
BF = jnp.bfloat16
F32 = jnp.float32


def sum_kernel(parts, out, total):
    total[...] = jnp.sum(parts[...].astype(F32), axis=0)
    rows = out.shape[1]
    for i in range(out.shape[0]):
        out[i] = total[i * rows:(i + 1) * rows, :].astype(BF)


def spread(block, axes, size):
    return lax.all_to_all(jnp.broadcast_to(block[None], (size,) + block.shape), axes, 0, 0)


def per_device(out_grad, hidden, segments, master, moment_one, moment_two, step_count, layer_one):
    n_zh, n_x, n_yh, n_yl = [lax.axis_size(a) for a in ("zh", "x", "yh", "yl")]
    n_y = n_yh * n_yl
    rows, width = master.shape
    tok_dev, units = hidden.shape
    all_tokens = tok_dev * n_zh * n_x * n_y

    with jax.named_scope("gather_grads"):
        full_grads = lax.all_gather(out_grad, ("zl", "c"), axis=0, tiled=True)

    with jax.named_scope("gather_weights"):
        pair = jnp.stack([master.astype(BF), layer_one])
        pair = spread(pair, "zh", n_zh)
        pair = spread(pair, ("yh", "yl"), n_y)
        pair = pair.transpose(2, 1, 0, 3, 4).reshape(2, n_zh * n_y * rows, width)
        last = spread(pair[0], "x", n_x)
        first = lax.all_gather(pair[1], "x", axis=0, tiled=False)
        full_grads, last = lax.optimization_barrier((full_grads, last))

    def in_order(w):
        return w.reshape(n_x, n_zh, n_y * rows, width).transpose(1, 0, 2, 3).reshape(units, width)

    with jax.named_scope("weights_of_tokens"):
        seg_row = segments[0]
        same_doc = (seg_row[:, None] == seg_row[None, :]).astype(F32)
        doc_len = jnp.sum(same_doc, axis=1)
        weight = tok_dev / DOCS / doc_len
        scaled = (full_grads.astype(F32) * weight[:, None]).astype(BF)

    with jax.named_scope("unit_order"):
        at = jnp.arange(units, dtype=jnp.int32)
        order = at.reshape(n_zh, n_x, n_yh, n_yl, rows).transpose(1, 3, 0, 2, 4).reshape(units)
        pick = (at[:, None] == order[None, :]).astype(BF)
        ordered = lax.dot_general(
            hidden, pick, (((1,), (0,)), ((), ())), preferred_element_type=F32
        ).astype(BF)

    with jax.named_scope("hidden_grad"):
        hidden_grad = lax.dot_general(
            scaled, in_order(last), (((1,), (1,)), ((), ())), preferred_element_type=F32
        )
        hidden_grad = hidden_grad.astype(BF)

    with jax.named_scope("gradient"):
        grad_local = lax.dot_general(
            ordered, scaled, (((0,), (0,)), ((), ())), preferred_element_type=F32
        ).astype(BF)
        parts = lax.all_to_all(
            grad_local.reshape(n_x * n_yl, units // (n_x * n_yl), width), ("x", "yl"), 0, 0
        )
        parts, hidden_grad = lax.optimization_barrier((parts, hidden_grad))
        vmem = pl.BlockSpec(memory_space=pltpu.VMEM)
        part = pl.pallas_call(
            sum_kernel,
            out_shape=jax.ShapeDtypeStruct((n_zh * n_yh, rows, width), BF),
            in_specs=[vmem],
            out_specs=vmem,
            scratch_shapes=[pltpu.VMEM((n_zh * n_yh * rows, width), F32)],
            compiler_params=pltpu.CompilerParams(vmem_limit_bytes=16 << 20),
        )(parts)
        parts = lax.all_to_all(part, ("zh", "yh"), 0, 0)
        parts, first = lax.optimization_barrier((parts, first))
        gradient = jnp.sum(parts.astype(F32), axis=0)

    with jax.named_scope("adamw"):
        gradient = gradient / all_tokens
        new_moment_one = 0.9 * moment_one + 0.1 * gradient
        new_moment_two = 0.95 * moment_two + 0.05 * gradient * gradient
        step_float = step_count.astype(F32)
        first_fix = 1.0 - jnp.power(F32(0.9), step_float)
        second_fix = 1.0 - jnp.power(F32(0.95), step_float)
        update = (
            new_moment_one / first_fix / (jnp.sqrt(new_moment_two / second_fix) + 1e-08)
            + 0.1 * master
        )
        new_master = master - 0.00015 * update
    return (
        hidden_grad,
        new_master,
        new_moment_one,
        new_moment_two,
        update,
        in_order(first),
    )


def solution(mesh):
    fine = Mesh(mesh.devices.reshape(3, 4, 4, 2, 4, 2), ("zh", "x", "yh", "yl", "zl", "c"))
    fsdp = ("zh", "x", "yh", "yl")
    tensor = ("zl", "c")
    in_specs = (
        P(fsdp + tensor, None),
        P(fsdp, tensor),
        P(fsdp, None),
        P(tensor + fsdp, None),
        P(tensor + fsdp, None),
        P(tensor + fsdp, None),
        P(),
        P(tensor + fsdp, None),
    )
    out_specs = (
        P(fsdp, tensor),
        P(tensor + fsdp, None),
        P(tensor + fsdp, None),
        P(tensor + fsdp, None),
        P(tensor + fsdp, None),
        P(tensor, None),
    )
    return jax.shard_map(
        per_device, mesh=fine, in_specs=in_specs, out_specs=out_specs, check_vma=False
    )
```

```python
import jax
import jax.numpy as jnp
from jax import lax
from jax.experimental import pallas as pl
from jax.experimental.pallas import tpu as pltpu
from jax.sharding import Mesh
from jax.sharding import PartitionSpec as P

DOCS = 8
BF = jnp.bfloat16
F32 = jnp.float32


def sum_kernel(parts, out, total):
    total[...] = jnp.sum(parts[...].astype(F32), axis=0)
    rows = out.shape[1]
    for i in range(out.shape[0]):
        out[i] = total[i * rows:(i + 1) * rows, :].astype(BF)


def spread(block, axes, size):
    return lax.all_to_all(jnp.broadcast_to(block[None], (size,) + block.shape), axes, 0, 0)


def per_device(out_grad, hidden, segments, master, moment_one, moment_two, step_count, layer_one):
    n_zh, n_x, n_yh, n_yl = [lax.axis_size(a) for a in ("zh", "x", "yh", "yl")]
    n_y = n_yh * n_yl
    rows, width = master.shape
    tok_dev, units = hidden.shape
    all_tokens = tok_dev * n_zh * n_x * n_y

    with jax.named_scope("gather_grads"):
        full_grads = lax.all_gather(out_grad, ("zl", "c"), axis=0, tiled=True)

    with jax.named_scope("gather_weights"):
        pair = jnp.stack([master.astype(BF), layer_one])
        pair = spread(pair, "zh", n_zh)
        pair = spread(pair, ("yh", "yl"), n_y)
        pair = pair.transpose(2, 1, 0, 3, 4).reshape(2, n_zh * n_y * rows, width)
        last = spread(pair[0], "x", n_x)
        first = lax.all_gather(pair[1], "x", axis=0, tiled=False)
    def in_order(w):
        return w.reshape(n_x, n_zh, n_y * rows, width).transpose(1, 0, 2, 3).reshape(units, width)

    with jax.named_scope("unit_order"):
        at = jnp.arange(units, dtype=jnp.int32)
        order = at.reshape(n_zh, n_x, n_yh, n_yl, rows).transpose(1, 3, 0, 2, 4).reshape(units)
        pick = (order[:, None] == at[None, :]).astype(BF)
        hidden_t = lax.dot_general(
            pick, hidden, (((1,), (1,)), ((), ())), preferred_element_type=F32
        ).astype(BF)

    full_grads, last, hidden_t = lax.optimization_barrier((full_grads, last, hidden_t))

    with jax.named_scope("weights_of_tokens"):
        seg_row = segments[0]
        same_doc = (seg_row[:, None] == seg_row[None, :]).astype(F32)
        doc_len = jnp.sum(same_doc, axis=1)
        weight = tok_dev / DOCS / doc_len
        scaled = (full_grads.astype(F32) * weight[:, None]).astype(BF)

    with jax.named_scope("hidden_grad"):
        hidden_grad = lax.dot_general(
            scaled, in_order(last), (((1,), (1,)), ((), ())), preferred_element_type=F32
        )
        hidden_grad = hidden_grad.astype(BF)

    with jax.named_scope("gradient"):
        grad_local = lax.dot_general(
            hidden_t, scaled, (((1,), (0,)), ((), ())), preferred_element_type=F32
        ).astype(BF)
        parts = lax.all_to_all(
            grad_local.reshape(n_x * n_yl, units // (n_x * n_yl), width), ("x", "yl"), 0, 0
        )
        parts, hidden_grad = lax.optimization_barrier((parts, hidden_grad))
        vmem = pl.BlockSpec(memory_space=pltpu.VMEM)
        part = pl.pallas_call(
            sum_kernel,
            out_shape=jax.ShapeDtypeStruct((n_zh * n_yh, rows, width), BF),
            in_specs=[vmem],
            out_specs=vmem,
            scratch_shapes=[pltpu.VMEM((n_zh * n_yh * rows, width), F32)],
            compiler_params=pltpu.CompilerParams(vmem_limit_bytes=16 << 20),
        )(parts)
        parts = lax.all_to_all(part, ("zh", "yh"), 0, 0)
        parts, first = lax.optimization_barrier((parts, in_order(first)))
        gradient = jnp.sum(parts.astype(F32), axis=0)

    with jax.named_scope("adamw"):
        gradient = gradient / all_tokens
        new_moment_one = 0.9 * moment_one + 0.1 * gradient
        new_moment_two = 0.95 * moment_two + 0.05 * gradient * gradient
        step_float = step_count.astype(F32)
        first_fix = 1.0 - jnp.power(F32(0.9), step_float)
        second_fix = 1.0 - jnp.power(F32(0.95), step_float)
        update = (
            new_moment_one / first_fix / (jnp.sqrt(new_moment_two / second_fix) + 1e-08)
            + 0.1 * master
        )
        new_master = master - 0.00015 * update
    return (
        hidden_grad,
        new_master,
        new_moment_one,
        new_moment_two,
        update,
        first,
    )


def solution(mesh):
    fine = Mesh(mesh.devices.reshape(3, 4, 4, 2, 4, 2), ("zh", "x", "yh", "yl", "zl", "c"))
    fsdp = ("zh", "x", "yh", "yl")
    tensor = ("zl", "c")
    in_specs = (
        P(fsdp + tensor, None),
        P(fsdp, tensor),
        P(fsdp, None),
        P(tensor + fsdp, None),
        P(tensor + fsdp, None),
        P(tensor + fsdp, None),
        P(),
        P(tensor + fsdp, None),
    )
    out_specs = (
        P(fsdp, tensor),
        P(tensor + fsdp, None),
        P(tensor + fsdp, None),
        P(tensor + fsdp, None),
        P(tensor + fsdp, None),
        P(tensor, None),
    )
    return jax.shard_map(
        per_device, mesh=fine, in_specs=in_specs, out_specs=out_specs, check_vma=False
    )
```

```python
import jax
import jax.numpy as jnp
from jax import lax
from jax.experimental import pallas as pl
from jax.experimental.pallas import tpu as pltpu
from jax.sharding import Mesh
from jax.sharding import PartitionSpec as P

DOCS = 8
BF = jnp.bfloat16
F32 = jnp.float32


def sum_kernel(parts, out, total):
    total[...] = jnp.sum(parts[...].astype(F32), axis=0)
    rows = out.shape[1]
    for i in range(out.shape[0]):
        out[i] = total[i * rows:(i + 1) * rows, :].astype(BF)


def spread(block, axes, size):
    return lax.all_to_all(jnp.broadcast_to(block[None], (size,) + block.shape), axes, 0, 0)


def per_device(out_grad, hidden, segments, master, moment_one, moment_two, step_count, layer_one):
    n_zh, n_x, n_yh, n_yl = [lax.axis_size(a) for a in ("zh", "x", "yh", "yl")]
    n_y = n_yh * n_yl
    rows, width = master.shape
    tok_dev, units = hidden.shape
    all_tokens = tok_dev * n_zh * n_x * n_y

    with jax.named_scope("gather_grads"):
        full_grads = lax.all_gather(out_grad, ("zl", "c"), axis=0, tiled=True)

    with jax.named_scope("gather_weights"):
        pair = jnp.stack([master.astype(BF), layer_one])
        pair = spread(pair, "zh", n_zh)
        pair = spread(pair, ("yh", "yl"), n_y)
        pair = pair.transpose(2, 1, 0, 3, 4).reshape(2, n_zh * n_y * rows, width)
        last = spread(pair[0], "x", n_x)
        first = lax.all_gather(pair[1], "x", axis=0, tiled=False)

    def in_order(w):
        return w.reshape(n_x, n_zh, n_y * rows, width).transpose(1, 0, 2, 3).reshape(units, width)

    with jax.named_scope("unit_order"):
        at = jnp.arange(units, dtype=jnp.int32)
        order = at.reshape(n_zh, n_x, n_yh, n_yl, rows).transpose(1, 3, 0, 2, 4).reshape(units)
        pick = (order[:, None] == at[None, :]).astype(BF)
        hidden_t = lax.dot_general(
            pick, hidden, (((1,), (1,)), ((), ())), preferred_element_type=F32
        ).astype(BF)

    full_grads, hidden_t = lax.optimization_barrier((full_grads, hidden_t))

    with jax.named_scope("weights_of_tokens"):
        seg_row = segments[0]
        same_doc = (seg_row[:, None] == seg_row[None, :]).astype(F32)
        doc_len = jnp.sum(same_doc, axis=1)
        weight = tok_dev / DOCS / doc_len
        scaled = (full_grads.astype(F32) * weight[:, None]).astype(BF)

    with jax.named_scope("gradient"):
        grad_local = lax.dot_general(
            hidden_t, scaled, (((1,), (0,)), ((), ())), preferred_element_type=F32
        ).astype(BF)
        grad_local, last = lax.optimization_barrier((grad_local, last))
        hidden_grad = lax.dot_general(
            scaled, in_order(last), (((1,), (1,)), ((), ())), preferred_element_type=F32
        )
        hidden_grad = hidden_grad.astype(BF)
        parts = lax.all_to_all(
            grad_local.reshape(n_x * n_yl, units // (n_x * n_yl), width), ("x", "yl"), 0, 0
        )
        parts, hidden_grad = lax.optimization_barrier((parts, hidden_grad))
        vmem = pl.BlockSpec(memory_space=pltpu.VMEM)
        part = pl.pallas_call(
            sum_kernel,
            out_shape=jax.ShapeDtypeStruct((n_zh * n_yh, rows, width), BF),
            in_specs=[vmem],
            out_specs=vmem,
            scratch_shapes=[pltpu.VMEM((n_zh * n_yh * rows, width), F32)],
            compiler_params=pltpu.CompilerParams(vmem_limit_bytes=16 << 20),
        )(parts)
        parts = lax.all_to_all(part, ("zh", "yh"), 0, 0)
        parts, first = lax.optimization_barrier((parts, in_order(first)))
        gradient = jnp.sum(parts.astype(F32), axis=0)

    with jax.named_scope("adamw"):
        gradient = gradient / all_tokens
        new_moment_one = 0.9 * moment_one + 0.1 * gradient
        new_moment_two = 0.95 * moment_two + 0.05 * gradient * gradient
        step_float = step_count.astype(F32)
        first_fix = 1.0 - jnp.power(F32(0.9), step_float)
        second_fix = 1.0 - jnp.power(F32(0.95), step_float)
        update = (
            new_moment_one / first_fix / (jnp.sqrt(new_moment_two / second_fix) + 1e-08)
            + 0.1 * master
        )
        new_master = master - 0.00015 * update
    return (
        hidden_grad,
        new_master,
        new_moment_one,
        new_moment_two,
        update,
        first,
    )


def solution(mesh):
    fine = Mesh(mesh.devices.reshape(3, 4, 4, 2, 4, 2), ("zh", "x", "yh", "yl", "zl", "c"))
    fsdp = ("zh", "x", "yh", "yl")
    tensor = ("zl", "c")
    in_specs = (
        P(fsdp + tensor, None),
        P(fsdp, tensor),
        P(fsdp, None),
        P(tensor + fsdp, None),
        P(tensor + fsdp, None),
        P(tensor + fsdp, None),
        P(),
        P(tensor + fsdp, None),
    )
    out_specs = (
        P(fsdp, tensor),
        P(tensor + fsdp, None),
        P(tensor + fsdp, None),
        P(tensor + fsdp, None),
        P(tensor + fsdp, None),
        P(tensor, None),
    )
    return jax.shard_map(
        per_device, mesh=fine, in_specs=in_specs, out_specs=out_specs, check_vma=False
    )
```
